32 devices in a mesh: seq: 8 (over y, x, core), head: 4 (over z).
Axes of the slice: x: 2, y: 2, z: 4, core: 2. Of those that a mesh axis runs over, the one named last changes fastest.
Arguments:
- q_rows: float32 [2048, 2048], P(('seq', 'head')), may hold values from -4 to 4
- k_rows: float32 [2048, 2048], P(('seq', 'head')), may hold values from -4 to 4
- v_rows: float32 [2048, 2048], P(('seq', 'head')), may hold values from -6 to 6
- step_sizes: float32 [8, 2048], P('head', 'seq'), may hold values from 0.1 to 1
- fast_weights: float32 [3, 8, 256, 512], P(None, 'head'), may hold values from -0.375 to 0.375
- norm_gain: float32 [2048], P('head'), may hold values from 0.1 to 1.9
- w_out: bfloat16 [2048, 4096], P('head'), may hold values from -0.125 to 0.125
Outputs:
- mixed_out: bfloat16 [2048, 4096], P(('seq', 'head'))
- new_weights: float32 [3, 8, 256, 512], P(None, 'head')
The draws below stay inside these ranges and needn't reach their ends.
All inputs are finite; a program needn't handle non-finite values.
Results may differ from the reference program's by a relative error of at most 0.005.
Values sent between devices are 32-bit elements; how exact they have to be, the bound alone decides.
A program may use at most 128 MiB of HBM per device.

```python
import math
import jax
import jax.numpy as jnp
from jax import lax

D = 4096
H = 8
DH = 256
HID = 512
WINDOW = 256
NS_ITERS = 3
TOKENS = 2048
HD = 2048


def drawn_pair(key):
    base_key = jax.random.fold_in(key, 7)
    subkeys = jax.random.split(base_key, 4)
    query_part = jnp.clip(jax.random.normal(subkeys[2], (TOKENS, HD), jnp.float32), -4.0, 4.0)
    key_part = jnp.clip(jax.random.normal(subkeys[3], (TOKENS, HD), jnp.float32), -4.0, 4.0)
    return (query_part, key_part)


def draw_q_rows(key, part):
    return drawn_pair(key)[0]


def draw_k_rows(key, part):
    return drawn_pair(key)[1]


def level_of(stream_key, dims, cuts, least, largest):
    factor_of, own = 1.0, jax.random.fold_in(stream_key, 6)
    for axis_at, parts in cuts:
        heights = jnp.exp(jax.random.uniform(jax.random.fold_in(own, axis_at), (parts,), jnp.float32, least / len(cuts), largest / len(cuts)))
        factor_of = factor_of * jnp.repeat(heights, dims[axis_at] // parts).reshape([-1 if axis == axis_at else 1 for axis in range(len(dims))])
    return factor_of


def bell_draw(rng, extent, scale, most, cuts=(), kind=jnp.bfloat16):
    values = jax.random.normal(rng, extent, jnp.float32) * scale
    if len(cuts) > 0:
        values = level_of(rng, extent, cuts, -0.22, 0.18) * values
    return jnp.clip(values, min=-most, max=most).astype(kind)


def setup_inputs(seed: int = 0) -> dict:
    key_list = jax.random.split(jax.random.key(seed), 8)
    q_rows = draw_q_rows(jax.random.fold_in(key_list[7], 71), 0)
    k_rows = draw_k_rows(jax.random.fold_in(key_list[7], 71), 0)
    v_rows = bell_draw(key_list[2], (TOKENS, HD), 1.0, 6.0, ((0, 32),), jnp.float32)
    step_sizes = jnp.clip(jnp.exp(math.log(1.0) - 2.3025851 * jax.random.uniform(key_list[3], (H, TOKENS), jnp.float32) ** level_of(key_list[3], (H, TOKENS), ((0, 4), (1, 8)), -0.2, 0.2)), 0.1, 1.0)
    fast_weights = bell_draw(key_list[4], (3, H, DH, HID), DH ** -0.5, 0.375, ((1, 4),), jnp.float32)
    norm_gain = jnp.clip(1.0 + 0.18 * jax.random.normal(key_list[5], (HD,), jnp.float32), 0.1, 1.9)
    w_out = bell_draw(key_list[6], (HD, D), HD ** -0.5, 0.125, ((0, 4),))
    return dict(q_rows=q_rows, k_rows=k_rows, v_rows=v_rows, step_sizes=step_sizes, fast_weights=fast_weights, norm_gain=norm_gain, w_out=w_out)


highest = lax.Precision.HIGHEST
epsilon = 1e-06
coef_linear = 3.4445
coef_square = -4.775
coef_cubic = 2.0315

def silu_parts(pre_act):
    sigmoid_gate = jax.nn.sigmoid(pre_act)
    return (pre_act * sigmoid_gate, sigmoid_gate)

def fast_gradients(key_heads, value_heads, step_sizes, weights):
    gate_pre = jnp.einsum('hnd,hdj->hnj', key_heads, weights[0], precision=highest)
    up_pre = jnp.einsum('hnd,hdj->hnj', key_heads, weights[2], precision=highest)
    active, sigmoid_gate = silu_parts(gate_pre)
    glu_out = active * up_pre
    upstream = -step_sizes[:, :, None] * value_heads
    grad_two = jnp.einsum('hnd,hnj->hdj', upstream, glu_out, precision=highest)
    upstream_glu = jnp.einsum('hnd,hdj->hnj', upstream, weights[1], precision=highest)
    grad_three = jnp.einsum('hnd,hnj->hdj', key_heads, upstream_glu * active, precision=highest)
    slope = sigmoid_gate * (1.0 + gate_pre * (1.0 - sigmoid_gate))
    grad_one = jnp.einsum('hnd,hnj->hdj', key_heads, upstream_glu * up_pre * slope, precision=highest)
    return jnp.stack([grad_one, grad_two, grad_three])

def orthogonalize(gradients):
    inverse_norm = 1.0 / (jnp.sqrt(lax.optimization_barrier(jnp.sum(gradients * gradients, axis=(2, 3), keepdims=True))) + epsilon)
    matrix = gradients * inverse_norm
    for iteration in range(NS_ITERS):
        gram_matrix = jnp.einsum('chdj,chej->chde', matrix, matrix, precision=highest)
        polynomial = coef_square * gram_matrix + coef_cubic * jnp.einsum('chde,chef->chdf', gram_matrix, gram_matrix, precision=highest)
        matrix = coef_linear * matrix + jnp.einsum('chde,chej->chdj', polynomial, matrix, precision=highest)
    return matrix

def renormalize(old_weights, candidate):
    target = jnp.sqrt(lax.optimization_barrier(jnp.sum(old_weights * old_weights, axis=2, keepdims=True)))
    current = jnp.sqrt(lax.optimization_barrier(jnp.sum(candidate * candidate, axis=2, keepdims=True))) + epsilon
    return candidate * (target / current)

def window_attention(queries, key_rows, value_rows):
    block_rows = math.gcd(TOKENS, 512)
    padding = jnp.zeros((WINDOW, H, DH), jnp.float32)
    padded_keys = jnp.concatenate([padding, key_rows], axis=0)
    padded_values = jnp.concatenate([padding, value_rows], axis=0)

    def one_block(first_row):
        query_block = lax.dynamic_slice_in_dim(queries, first_row, block_rows, 0)
        key_block = lax.dynamic_slice_in_dim(padded_keys, first_row, block_rows + WINDOW, 0)
        value_block = lax.dynamic_slice_in_dim(padded_values, first_row, block_rows + WINDOW, 0)
        query_pos = first_row + jnp.arange(block_rows, dtype=jnp.int32)
        key_pos = first_row - WINDOW + jnp.arange(block_rows + WINDOW, dtype=jnp.int32)
        allowed = (key_pos[None, :] <= query_pos[:, None]) & (key_pos[None, :] > query_pos[:, None] - WINDOW) & (key_pos[None, :] >= 0)
        scores = jnp.einsum('qhd,khd->hqk', query_block, key_block, precision=highest) / math.sqrt(DH)
        scores = jnp.where(allowed[None], scores, -1e+30)
        highest_score = lax.optimization_barrier(jnp.max(scores, axis=-1, keepdims=True))
        expo = jnp.exp(scores - highest_score)
        attention_weights = expo / lax.optimization_barrier(jnp.sum(expo, axis=-1, keepdims=True))
        return jnp.einsum('hqk,khd->qhd', attention_weights, value_block, precision=highest)
    starts = jnp.arange(TOKENS // block_rows, dtype=jnp.int32) * block_rows
    result = lax.map(one_block, starts)
    return result.reshape(TOKENS, H, DH)

def reference(q_rows, k_rows, v_rows, step_sizes, fast_weights, norm_gain, w_out):
    queries = q_rows.reshape(TOKENS, H, DH)
    key_rows = k_rows.reshape(TOKENS, H, DH)
    value_rows = v_rows.reshape(TOKENS, H, DH)
    gradients = fast_gradients(key_rows.transpose(1, 0, 2), value_rows.transpose(1, 0, 2), step_sizes, fast_weights)
    orthogonal = orthogonalize(gradients)
    new_weights = renormalize(fast_weights, fast_weights - orthogonal)
    query_heads = queries.transpose(1, 0, 2)
    gate_pre = jnp.einsum('hnd,hdj->hnj', query_heads, new_weights[0], precision=highest)
    up_pre = jnp.einsum('hnd,hdj->hnj', query_heads, new_weights[2], precision=highest)
    active, sigmoid_gate = silu_parts(gate_pre)
    fast_out = jnp.einsum('hnj,hdj->hnd', active * up_pre, new_weights[1], precision=highest)
    fast_out = fast_out * lax.rsqrt(lax.optimization_barrier(jnp.mean(fast_out * fast_out, axis=-1, keepdims=True)) + epsilon)
    fast_out = fast_out * norm_gain.reshape(H, 1, DH)
    attended = window_attention(queries, key_rows, value_rows)
    combined = (fast_out.transpose(1, 0, 2) + attended).reshape(TOKENS, HD).astype(jnp.bfloat16)
    mixed_out = jnp.dot(combined, w_out, preferred_element_type=jnp.float32).astype(jnp.bfloat16)
    return (mixed_out, new_weights)
```

```python
import functools
import math

import jax
import jax.numpy as jnp
from jax import lax
from jax.experimental import pallas as pl
from jax.experimental.pallas import tpu as pltpu
from jax.sharding import PartitionSpec as P

WINDOW = 256
NS_ITERS = 3

epsilon = 1e-06
coef_linear = 3.4445
coef_square = -4.775
coef_cubic = 2.0315

MESH = pl.DeviceIdType.MESH
f32, bf16 = jnp.float32, jnp.bfloat16


def dot(a, b, dims=((1,), (0,))):
    return lax.dot_general(
        a.astype(bf16), b.astype(bf16), (dims, ((), ())), preferred_element_type=f32
    )


NT, TN = ((1,), (1,)), ((0,), (0,))


def split(x):
    high = x.astype(bf16)
    return high, (x - high.astype(f32)).astype(bf16)


def dot3(a, b, dims=((1,), (0,))):
    a_high, a_low = a if isinstance(a, tuple) else split(a)
    b_high, b_low = b if isinstance(b, tuple) else split(b)
    small = dot(a_high, b_low, dims) + dot(a_low, b_high, dims)
    return dot(a_high, b_high, dims) + small


def kernel(
    ns, nz, chunks,
    q_in, k_in, v_in, step_ref, fw_in, gain_ref, w_in,
    out_ref, new_ref,
    qkv, halo, fw, w_out, grads, swap, rs_in, full, new, comb, part, up, down,
    a2a_send, a2a_recv, own_sem, halo_send, halo_recv, load_sem,
    swap_send, swap_recv, rs_send, rs_recv, ag_send, ag_recv,
    new_send, new_recv, store_sem, up_send, up_recv, down_send, down_recv,
):
    s, z = lax.axis_index("seq"), lax.axis_index("head")
    length, width = qkv.shape[1], qkv.shape[2]
    rows = length // nz
    head_dim, hidden = fw.shape[2], fw.shape[3]
    bits = ns.bit_length() - 1
    core = lax.rem(s, 2)

    def bit_of(bit):
        return lax.rem(s // (1 << bit), 2)

    def across(bit):
        return s + (1 - 2 * bit_of(bit)) * (1 << bit)

    def at(seq, head):
        return (seq, head)

    later, earlier = lax.rem(s + 1, ns), lax.rem(s + ns - 1, ns)
    loads = [
        pltpu.make_async_copy(fw_in, fw, load_sem.at[0]),
        pltpu.make_async_copy(w_in, w_out, load_sem.at[1]),
    ]
    loads[0].start()
    own = []
    for array, source in ((1, k_in), (2, v_in), (0, q_in)):
        copy = pltpu.make_async_copy(
            source.at[:, pl.ds(pl.multiple_of(z * width, width), width)],
            qkv.at[array, pl.ds(pl.multiple_of(z * rows, rows), rows)],
            own_sem.at[array],
        )
        copy.start()
        own.append(copy)

    barrier = pltpu.get_barrier_semaphore()
    partners = [at(s, lax.rem(z + off, nz)) for off in range(1, nz)]
    partners += [at(across(bit), z) for bit in range(bits)]
    partners += [at(later, z), at(earlier, z)]
    for partner in partners:
        pl.semaphore_signal(barrier, inc=1, device_id=partner, device_id_type=MESH)
    pl.semaphore_wait(barrier, len(partners))

    a2a = {}

    def exchange(array, source):
        for off in range(1, nz):
            target = lax.rem(z + off, nz)
            copy = pltpu.make_async_remote_copy(
                source.at[:, pl.ds(pl.multiple_of(target * width, width), width)],
                qkv.at[array, pl.ds(pl.multiple_of(z * rows, rows), rows)],
                a2a_send.at[array, off - 1],
                a2a_recv.at[array, off - 1],
                device_id=at(s, target),
                device_id_type=MESH,
            )
            copy.start()
            a2a[array, off] = copy

    exchange(1, k_in)
    exchange(2, v_in)
    loads[1].start()

    def arrived(array):
        for off in range(1, nz):
            a2a[array, off].wait_recv()

    halos = []

    def send_halo(which):
        copy = pltpu.make_async_remote_copy(
            qkv.at[which + 1], halo.at[which], halo_send.at[which], halo_recv.at[which],
            device_id=at(later, z), device_id_type=MESH,
        )
        copy.start()
        halos.append(copy)

    own[0].wait()
    arrived(1)
    send_halo(0)
    loads[0].wait()
    head_cols = lambda h: pl.ds(pl.multiple_of(h * head_dim, head_dim), head_dim)

    other = 1 - core
    forward = []
    for h in (other, core):
        key = split(qkv[1, :, head_cols(h)])
        gate = dot3(key, fw[0, h])
        up_pre = dot3(key, fw[2, h])
        sig = jax.nn.sigmoid(gate)
        active = gate * sig
        glu = active * up_pre
        slope = up_pre * sig * (1.0 + gate * (1.0 - sig))
        forward.append((h, key, active, glu, slope))
    own[1].wait()
    arrived(2)
    send_halo(1)
    exchange(0, q_in)
    swaps = []
    for turn, (h, key, active, glu, slope) in enumerate(forward):
        upstream = split(-(qkv[2, :, head_cols(h)].T) * step_ref[pl.ds(h, 1), :])
        back = dot3(upstream, fw[1, h], TN)
        for m, value in (
            (1, lambda: dot3(upstream, glu)),
            (2, lambda: dot3(key, back * active, TN)),
            (0, lambda: dot3(key, back * slope, TN)),
        ):
            grads[turn, pl.ds(m * head_dim, head_dim)] = value()
            if turn == 0:
                copy = pltpu.make_async_remote_copy(
                    grads.at[0, pl.ds(m * head_dim, head_dim)],
                    swap.at[pl.ds(m * head_dim, head_dim)],
                    swap_send.at[m], swap_recv.at[m],
                    device_id=at(across(0), z), device_id_type=MESH,
                )
                copy.start()
                swaps.append((m, copy))
    for m, copy in swaps:
        copy.wait()
        block = pl.ds(m * head_dim, head_dim)
        grads[1, block] = grads[1, block] + swap[block]

    total_rows = 3 * head_dim
    half_cols = hidden // 2
    orders = [list(range(1, bits)), list(range(bits - 1, 0, -1))]
    lo = [0, 0]
    spans = [[], []]
    size, base = total_rows, 0

    def attend(h):
        query = qkv[0, :, head_cols(h)]
        scores = jnp.concatenate(
            [
                dot(query, halo[0, :, head_cols(h)], NT),
                dot(query, qkv[1, :, head_cols(h)], NT),
            ],
            axis=1,
        ) * (1.0 / math.sqrt(head_dim))
        query_pos = lax.broadcasted_iota(jnp.int32, scores.shape, 0)
        key_pos = lax.broadcasted_iota(jnp.int32, scores.shape, 1) - length
        allowed = (
            (key_pos <= query_pos) & (key_pos > query_pos - WINDOW) & (key_pos >= -s * length)
        )
        scores = jnp.where(allowed, scores, -1e30)
        expo = jnp.exp(scores - jnp.max(scores, axis=-1, keepdims=True))
        weights = expo / jnp.sum(expo, axis=-1, keepdims=True)
        return dot(weights[:, :length], halo[1, :, head_cols(h)]) + dot(
            weights[:, length:], qkv[2, :, head_cols(h)]
        )

    attended = []

    def attention():
        own[2].wait()
        arrived(0)
        for copy in halos:
            copy.wait()
        for h in (core, other):
            attended.append(attend(h))

    for step in range(bits - 1):
        size //= 2
        pending = []
        for side in range(2):
            bit = orders[side][step]
            mine = bit_of(bit)
            cols = pl.ds(side * half_cols, half_cols)
            give = pl.multiple_of(lo[side] + (1 - mine) * size, 8)
            copy = pltpu.make_async_remote_copy(
                grads.at[1, pl.ds(give, size), cols],
                rs_in.at[pl.ds(base, size), cols],
                rs_send.at[side, step], rs_recv.at[side, step],
                device_id=at(across(bit), z), device_id_type=MESH,
            )
            copy.start()
            pending.append(copy)
            spans[side].append((lo[side], lo[side] + mine * size, size, bit))
            lo[side] = lo[side] + mine * size
        if step == min(1, bits - 2):
            attention()
        for side in range(2):
            pending[side].wait()
            cols = pl.ds(side * half_cols, half_cols)
            keep = pl.ds(pl.multiple_of(lo[side], 8), size)
            total = grads[1, keep, cols] + rs_in[pl.ds(base, size), cols]
            if step == bits - 2:
                full[keep, cols] = total
            else:
                grads[1, keep, cols] = total
        base += size
    for step in range(bits - 2, -1, -1):
        pending = []
        for side in range(2):
            _, start, size, bit = spans[side][step]
            block = full.at[
                pl.ds(pl.multiple_of(start, 8), size), pl.ds(side * half_cols, half_cols)
            ]
            copy = pltpu.make_async_remote_copy(
                block, block, ag_send.at[side, step], ag_recv.at[side, step],
                device_id=at(across(bit), z), device_id_type=MESH,
            )
            copy.start()
            pending.append(copy)
        for copy in pending:
            copy.wait()

    mats = []
    for m in range(3):
        g = full[pl.ds(m * head_dim, head_dim)]
        mats.append(g * (1.0 / (jnp.sqrt(jnp.sum(g * g)) + epsilon)))
    for _ in range(NS_ITERS):
        pairs = [split(x) for x in mats]
        grams = [dot3(x, x, NT) for x in pairs]
        squares = [split(a) for a in grams]
        polys = [coef_square * a + coef_cubic * dot3(b, b) for a, b in zip(grams, squares)]
        mats = [coef_linear * x + dot3(p, y) for p, x, y in zip(polys, mats, pairs)]
    news = []
    stores = []
    for m in (0, 2, 1):
        old = fw[m, core]
        cand = old - mats[m]
        target = jnp.sqrt(jnp.sum(old * old, axis=0, keepdims=True))
        current = jnp.sqrt(jnp.sum(cand * cand, axis=0, keepdims=True)) + epsilon
        new[m, core] = cand * (target / current)
        copy = pltpu.make_async_remote_copy(
            new.at[m, core], new.at[m, core], new_send.at[m], new_recv.at[m],
            device_id=at(across(0), z), device_id_type=MESH,
        )
        copy.start()
        news.append(copy)
        copy = pltpu.make_async_copy(new.at[m, core], new_ref.at[m, core], store_sem.at[0, m])
        copy.start()
        stores.append(copy)

    def mix(h, attended_h):
        query = split(qkv[0, :, head_cols(h)])
        gate = dot3(query, new[0, h])
        up_pre = dot3(query, new[2, h])
        fast = dot3(gate * jax.nn.sigmoid(gate) * up_pre, new[1, h], NT)
        fast = fast * lax.rsqrt(jnp.mean(fast * fast, axis=-1, keepdims=True) + epsilon)
        fast = fast * gain_ref[:, head_cols(h)]
        comb[:, head_cols(h)] = (fast + attended_h).astype(bf16)

    mix(core, attended[0])
    for copy in news:
        copy.wait()
    for m in range(3):
        copy = pltpu.make_async_copy(new.at[m, other], new_ref.at[m, other], store_sem.at[1, m])
        copy.start()
        stores.append(copy)
    mix(other, attended[1])

    loads[1].wait()
    columns = w_out.shape[1]
    wide = columns // chunks
    above, below = lax.rem(z + 1, nz), lax.rem(z + nz - 1, nz)

    def flow(d, q, upward):
        cols = pl.ds(q * wide, wide)
        landing, send, recv = (up, up_send, up_recv) if upward else (down, down_send, down_recv)
        return pltpu.make_async_remote_copy(
            part.at[d, :, cols], landing.at[d, :, cols], send.at[d, q], recv.at[d, q],
            device_id=at(s, above if upward else below), device_id_type=MESH,
        )

    def moves(d, upward):
        return (z < d) if upward else (z > d)

    def comes(d, upward):
        return ((z > 0) & (z <= d)) if upward else ((z < nz - 1) & (z >= d))

    order = []
    for i in range(nz):
        order += [(nz - 1 - i, True), (i, False)]

    for q in range(chunks):
        cols = pl.ds(q * wide, wide)
        whole = dot(comb[...], w_out[:, cols])
        for d in range(nz):
            part[d, :, cols] = whole[d * rows : (d + 1) * rows]
        for d, upward in order:
            first = (z == 0) if upward else (z == nz - 1)

            @pl.when(first & moves(d, upward))
            def _():
                flow(d, q, upward).start()

    for q in range(chunks):
        cols = pl.ds(q * wide, wide)
        for d, upward in order:
            landing = up if upward else down

            @pl.when(comes(d, upward))
            def _():
                flow(d, q, upward).wait_recv()
                part[d, :, cols] = part[d, :, cols] + landing[d, :, cols]

                @pl.when(moves(d, upward))
                def _():
                    flow(d, q, upward).start()

        out_ref[:, cols] = part[z, :, cols].astype(out_ref.dtype)

    for q in range(chunks):
        for d, upward in order:

            @pl.when(moves(d, upward))
            def _():
                flow(d, q, upward).wait_send()

    for copy in stores:
        copy.wait()
    for copy in a2a.values():
        copy.wait_send()


def solution(mesh):
    ns, nz = mesh.shape["seq"], mesh.shape["head"]
    chunks = 4

    def local(q_rows, k_rows, v_rows, step_sizes, fast_weights, norm_gain, w_out):
        mats, heads, head_dim, hidden = fast_weights.shape
        width, length = heads * head_dim, q_rows.shape[0] * nz
        rows, columns = q_rows.shape[0], w_out.shape[1]
        bits = ns.bit_length() - 1
        dma = pltpu.SemaphoreType.DMA
        anywhere = pl.BlockSpec(memory_space=pl.ANY)
        vmem = pl.BlockSpec(memory_space=pltpu.VMEM)
        return pl.pallas_call(
            functools.partial(kernel, ns, nz, chunks),
            out_shape=(
                jax.ShapeDtypeStruct((rows, columns), bf16),
                jax.ShapeDtypeStruct(fast_weights.shape, f32),
            ),
            in_specs=[anywhere, anywhere, anywhere, vmem, anywhere, vmem, anywhere],
            out_specs=(vmem, anywhere),
            scratch_shapes=[
                pltpu.VMEM((3, length, width), f32),
                pltpu.VMEM((2, length, width), f32),
                pltpu.VMEM(fast_weights.shape, f32),
                pltpu.VMEM(w_out.shape, w_out.dtype),
                pltpu.VMEM((2, mats * head_dim, hidden), f32),
                pltpu.VMEM((mats * head_dim, hidden), f32),
                pltpu.VMEM((mats * head_dim, hidden), f32),
                pltpu.VMEM((mats * head_dim, hidden), f32),
                pltpu.VMEM(fast_weights.shape, f32),
                pltpu.VMEM((length, width), bf16),
                pltpu.VMEM((nz, rows, columns), f32),
                pltpu.VMEM((nz, rows, columns), f32),
                pltpu.VMEM((nz, rows, columns), f32),
                dma((3, nz - 1)), dma((3, nz - 1)), dma((3,)), dma((2,)), dma((2,)), dma((2,)),
                dma((3,)), dma((3,)),
                dma((2, bits - 1)), dma((2, bits - 1)), dma((2, bits - 1)), dma((2, bits - 1)),
                dma((3,)), dma((3,)), dma((2, 3)),
                dma((nz, chunks)), dma((nz, chunks)), dma((nz, chunks)), dma((nz, chunks)),
            ],
            compiler_params=pltpu.CompilerParams(
                collective_id=0, has_side_effects=True, vmem_limit_bytes=56 * 2**20
            ),
        )(
            q_rows, k_rows, v_rows, step_sizes, fast_weights,
            norm_gain.reshape(1, -1), w_out,
        )

    return jax.shard_map(
        local,
        mesh=mesh,
        in_specs=(
            P(("seq", "head"), None),
            P(("seq", "head"), None),
            P(("seq", "head"), None),
            P("head", "seq"),
            P(None, "head", None, None),
            P("head"),
            P("head", None),
        ),
        out_specs=(P(("seq", "head"), None), P(None, "head", None, None)),
        check_vma=False,
    )
```

```python
import functools
import math

import jax
import jax.numpy as jnp
from jax import lax
from jax.experimental import pallas as pl
from jax.experimental.pallas import tpu as pltpu
from jax.sharding import PartitionSpec as P

WINDOW = 256
NS_ITERS = 3

epsilon = 1e-06
coef_linear = 3.4445
coef_square = -4.775
coef_cubic = 2.0315

MESH = pl.DeviceIdType.MESH
f32, bf16 = jnp.float32, jnp.bfloat16


def dot(a, b, dims=((1,), (0,))):
    return lax.dot_general(
        a.astype(bf16), b.astype(bf16), (dims, ((), ())), preferred_element_type=f32
    )


NT, TN = ((1,), (1,)), ((0,), (0,))


def split(x):
    high = x.astype(bf16)
    return high, (x - high.astype(f32)).astype(bf16)


def dot3(a, b, dims=((1,), (0,))):
    a_high, a_low = a if isinstance(a, tuple) else split(a)
    b_high, b_low = b if isinstance(b, tuple) else split(b)
    small = dot(a_high, b_low, dims) + dot(a_low, b_high, dims)
    return dot(a_high, b_high, dims) + small


def kernel(
    ns, nz, chunks,
    q_in, k_in, v_in, step_ref, fw_in, gain_ref, w_in,
    out_ref, new_ref,
    qkv, halo, fw, w_out, grads, swap, rs_in, full, new, comb, part, up, down,
    a2a_send, a2a_recv, own_sem, halo_send, halo_recv, load_sem,
    swap_send, swap_recv, rs_send, rs_recv, ag_send, ag_recv,
    new_send, new_recv, store_sem, up_send, up_recv, down_send, down_recv,
):
    s, z = lax.axis_index("seq"), lax.axis_index("head")
    length, width = qkv.shape[1], qkv.shape[2]
    rows = length // nz
    head_dim, hidden = fw.shape[2], fw.shape[3]
    bits = ns.bit_length() - 1
    core = lax.rem(s, 2)

    def bit_of(bit):
        return lax.rem(s // (1 << bit), 2)

    def across(bit):
        return s + (1 - 2 * bit_of(bit)) * (1 << bit)

    def at(seq, head):
        return (seq, head)

    later, earlier = lax.rem(s + 1, ns), lax.rem(s + ns - 1, ns)
    loads = [
        pltpu.make_async_copy(fw_in, fw, load_sem.at[0]),
        pltpu.make_async_copy(w_in, w_out, load_sem.at[1]),
    ]
    loads[0].start()
    own = []
    for array, source in ((1, k_in), (2, v_in), (0, q_in)):
        copy = pltpu.make_async_copy(
            source.at[:, pl.ds(pl.multiple_of(z * width, width), width)],
            qkv.at[array, pl.ds(pl.multiple_of(z * rows, rows), rows)],
            own_sem.at[array],
        )
        copy.start()
        own.append(copy)

    barrier = pltpu.get_barrier_semaphore()
    partners = [at(s, lax.rem(z + off, nz)) for off in range(1, nz)]
    partners += [at(across(bit), z) for bit in range(bits)]
    partners += [at(later, z), at(earlier, z)]
    for partner in partners:
        pl.semaphore_signal(barrier, inc=1, device_id=partner, device_id_type=MESH)
    pl.semaphore_wait(barrier, len(partners))

    a2a = {}

    def exchange(array, source):
        for off in range(1, nz):
            target = lax.rem(z + off, nz)
            copy = pltpu.make_async_remote_copy(
                source.at[:, pl.ds(pl.multiple_of(target * width, width), width)],
                qkv.at[array, pl.ds(pl.multiple_of(z * rows, rows), rows)],
                a2a_send.at[array, off - 1],
                a2a_recv.at[array, off - 1],
                device_id=at(s, target),
                device_id_type=MESH,
            )
            copy.start()
            a2a[array, off] = copy

    exchange(1, k_in)
    exchange(2, v_in)
    loads[1].start()

    def arrived(array):
        for off in range(1, nz):
            a2a[array, off].wait_recv()

    halos = []

    def send_halo(which):
        copy = pltpu.make_async_remote_copy(
            qkv.at[which + 1], halo.at[which], halo_send.at[which], halo_recv.at[which],
            device_id=at(later, z), device_id_type=MESH,
        )
        copy.start()
        halos.append(copy)

    own[0].wait()
    arrived(1)
    send_halo(0)
    loads[0].wait()
    head_cols = lambda h: pl.ds(pl.multiple_of(h * head_dim, head_dim), head_dim)

    other = 1 - core
    forward = []
    for h in (other, core):
        key = split(qkv[1, :, head_cols(h)])
        gate = dot3(key, fw[0, h])
        up_pre = dot3(key, fw[2, h])
        sig = jax.nn.sigmoid(gate)
        active = gate * sig
        glu = active * up_pre
        slope = up_pre * sig * (1.0 + gate * (1.0 - sig))
        forward.append((h, key, active, glu, slope))
    own[1].wait()
    arrived(2)
    send_halo(1)
    exchange(0, q_in)
    swaps = []
    for turn, (h, key, active, glu, slope) in enumerate(forward):
        upstream = split(-(qkv[2, :, head_cols(h)].T) * step_ref[pl.ds(h, 1), :])
        back = dot3(upstream, fw[1, h], TN)
        for m, value in (
            (1, lambda: dot3(upstream, glu)),
            (2, lambda: dot3(key, back * active, TN)),
            (0, lambda: dot3(key, back * slope, TN)),
        ):
            grads[turn, pl.ds(m * head_dim, head_dim)] = value()
            if turn == 0:
                copy = pltpu.make_async_remote_copy(
                    grads.at[0, pl.ds(m * head_dim, head_dim)],
                    swap.at[pl.ds(m * head_dim, head_dim)],
                    swap_send.at[m], swap_recv.at[m],
                    device_id=at(across(0), z), device_id_type=MESH,
                )
                copy.start()
                swaps.append((m, copy))
    for m, copy in swaps:
        copy.wait()
        block = pl.ds(m * head_dim, head_dim)
        grads[1, block] = grads[1, block] + swap[block]

    total_rows = 3 * head_dim
    half_cols = hidden // 2
    orders = [list(range(1, bits)), list(range(bits - 1, 0, -1))]
    lo = [0, 0]
    spans = [[], []]
    size, base = total_rows, 0

    def attend(h):
        query = qkv[0, :, head_cols(h)]
        scores = jnp.concatenate(
            [
                dot(query, halo[0, :, head_cols(h)], NT),
                dot(query, qkv[1, :, head_cols(h)], NT),
            ],
            axis=1,
        ) * (1.0 / math.sqrt(head_dim))
        query_pos = lax.broadcasted_iota(jnp.int32, scores.shape, 0)
        key_pos = lax.broadcasted_iota(jnp.int32, scores.shape, 1) - length
        allowed = (
            (key_pos <= query_pos) & (key_pos > query_pos - WINDOW) & (key_pos >= -s * length)
        )
        scores = jnp.where(allowed, scores, -1e30)
        expo = jnp.exp(scores - jnp.max(scores, axis=-1, keepdims=True))
        weights = expo / jnp.sum(expo, axis=-1, keepdims=True)
        return dot(weights[:, :length], halo[1, :, head_cols(h)]) + dot(
            weights[:, length:], qkv[2, :, head_cols(h)]
        )

    attended = []

    def attention():
        own[2].wait()
        arrived(0)
        for copy in halos:
            copy.wait()
        for h in (core, other):
            attended.append(attend(h))

    for step in range(bits - 1):
        size //= 2
        pending = []
        for side in range(2):
            bit = orders[side][step]
            mine = bit_of(bit)
            cols = pl.ds(side * half_cols, half_cols)
            give = pl.multiple_of(lo[side] + (1 - mine) * size, 8)
            copy = pltpu.make_async_remote_copy(
                grads.at[1, pl.ds(give, size), cols],
                rs_in.at[pl.ds(base, size), cols],
                rs_send.at[side, step], rs_recv.at[side, step],
                device_id=at(across(bit), z), device_id_type=MESH,
            )
            copy.start()
            pending.append(copy)
            spans[side].append((lo[side], lo[side] + mine * size, size, bit))
            lo[side] = lo[side] + mine * size
        if step == min(1, bits - 2):
            attention()
        for side in range(2):
            pending[side].wait()
            cols = pl.ds(side * half_cols, half_cols)
            keep = pl.ds(pl.multiple_of(lo[side], 8), size)
            total = grads[1, keep, cols] + rs_in[pl.ds(base, size), cols]
            if step == bits - 2:
                full[keep, cols] = total
            else:
                grads[1, keep, cols] = total
        base += size
    for step in range(bits - 2, -1, -1):
        pending = []
        for side in range(2):
            _, start, size, bit = spans[side][step]
            block = full.at[
                pl.ds(pl.multiple_of(start, 8), size), pl.ds(side * half_cols, half_cols)
            ]
            copy = pltpu.make_async_remote_copy(
                block, block, ag_send.at[side, step], ag_recv.at[side, step],
                device_id=at(across(bit), z), device_id_type=MESH,
            )
            copy.start()
            pending.append(copy)
        for copy in pending:
            copy.wait()

    mats = []
    for m in range(3):
        g = full[pl.ds(m * head_dim, head_dim)]
        mats.append(g * (1.0 / (jnp.sqrt(jnp.sum(g * g)) + epsilon)))
    for _ in range(NS_ITERS):
        pairs = [split(x) for x in mats]
        grams = [dot3(x, x, NT) for x in pairs]
        squares = [split(a) for a in grams]
        polys = [coef_square * a + coef_cubic * dot3(b, b) for a, b in zip(grams, squares)]
        mats = [coef_linear * x + dot3(p, y) for p, x, y in zip(polys, mats, pairs)]
    news = []
    stores = []
    for m in (0, 2, 1):
        old = fw[m, core]
        cand = old - mats[m]
        target = jnp.sqrt(jnp.sum(old * old, axis=0, keepdims=True))
        current = jnp.sqrt(jnp.sum(cand * cand, axis=0, keepdims=True)) + epsilon
        new[m, core] = cand * (target / current)
        copy = pltpu.make_async_remote_copy(
            new.at[m, core], new.at[m, core], new_send.at[m], new_recv.at[m],
            device_id=at(across(0), z), device_id_type=MESH,
        )
        copy.start()
        news.append(copy)
        copy = pltpu.make_async_copy(new.at[m, core], new_ref.at[m, core], store_sem.at[0, m])
        copy.start()
        stores.append(copy)

    def mix(h, attended_h):
        query = split(qkv[0, :, head_cols(h)])
        gate = dot3(query, new[0, h])
        up_pre = dot3(query, new[2, h])
        fast = dot3(gate * jax.nn.sigmoid(gate) * up_pre, new[1, h], NT)
        fast = fast * lax.rsqrt(jnp.mean(fast * fast, axis=-1, keepdims=True) + epsilon)
        fast = fast * gain_ref[:, head_cols(h)]
        comb[:, head_cols(h)] = (fast + attended_h).astype(bf16)

    mix(core, attended[0])
    for copy in news:
        copy.wait()
    for m in range(3):
        copy = pltpu.make_async_copy(new.at[m, other], new_ref.at[m, other], store_sem.at[1, m])
        copy.start()
        stores.append(copy)
    mix(other, attended[1])

    loads[1].wait()
    columns = w_out.shape[1]
    wide = columns // chunks
    above, below = lax.rem(z + 1, nz), lax.rem(z + nz - 1, nz)

    def flow(d, q, upward):
        cols = pl.ds(pl.multiple_of(q * wide, wide), wide)
        landing, send, recv = (up, up_send, up_recv) if upward else (down, down_send, down_recv)
        return pltpu.make_async_remote_copy(
            part.at[d, :, cols], landing.at[d, :, cols], send.at[d, q], recv.at[d, q],
            device_id=at(s, above if upward else below), device_id_type=MESH,
        )

    def moves(d, upward):
        return (z < d) if upward else (z > d)

    def comes(d, upward):
        return ((z > 0) & (z <= d)) if upward else ((z < nz - 1) & (z >= d))

    order = []
    for i in range(nz):
        order += [(nz - 1 - i, True), (i, False)]

    @pl.loop(0, chunks)
    def _(q):
        cols = pl.ds(pl.multiple_of(q * wide, wide), wide)
        whole = dot(comb[...], w_out[:, cols])
        for d in range(nz):
            part[d, :, cols] = whole[d * rows : (d + 1) * rows]
        for d, upward in order:
            first = (z == 0) if upward else (z == nz - 1)

            @pl.when(first & moves(d, upward))
            def _():
                flow(d, q, upward).start()

    @pl.loop(0, chunks)
    def _(q):
        cols = pl.ds(pl.multiple_of(q * wide, wide), wide)
        for d, upward in order:
            landing = up if upward else down

            @pl.when(comes(d, upward))
            def _():
                flow(d, q, upward).wait_recv()
                part[d, :, cols] = part[d, :, cols] + landing[d, :, cols]

                @pl.when(moves(d, upward))
                def _():
                    flow(d, q, upward).start()

        out_ref[:, cols] = part[z, :, cols].astype(out_ref.dtype)

    @pl.loop(0, chunks)
    def _(q):
        for d, upward in order:

            @pl.when(moves(d, upward))
            def _():
                flow(d, q, upward).wait_send()

    for copy in stores:
        copy.wait()
    for copy in a2a.values():
        copy.wait_send()


def solution(mesh):
    ns, nz = mesh.shape["seq"], mesh.shape["head"]
    chunks = 8

    def local(q_rows, k_rows, v_rows, step_sizes, fast_weights, norm_gain, w_out):
        mats, heads, head_dim, hidden = fast_weights.shape
        width, length = heads * head_dim, q_rows.shape[0] * nz
        rows, columns = q_rows.shape[0], w_out.shape[1]
        bits = ns.bit_length() - 1
        dma = pltpu.SemaphoreType.DMA
        anywhere = pl.BlockSpec(memory_space=pl.ANY)
        vmem = pl.BlockSpec(memory_space=pltpu.VMEM)
        return pl.pallas_call(
            functools.partial(kernel, ns, nz, chunks),
            out_shape=(
                jax.ShapeDtypeStruct((rows, columns), bf16),
                jax.ShapeDtypeStruct(fast_weights.shape, f32),
            ),
            in_specs=[anywhere, anywhere, anywhere, vmem, anywhere, vmem, anywhere],
            out_specs=(vmem, anywhere),
            scratch_shapes=[
                pltpu.VMEM((3, length, width), f32),
                pltpu.VMEM((2, length, width), f32),
                pltpu.VMEM(fast_weights.shape, f32),
                pltpu.VMEM(w_out.shape, w_out.dtype),
                pltpu.VMEM((2, mats * head_dim, hidden), f32),
                pltpu.VMEM((mats * head_dim, hidden), f32),
                pltpu.VMEM((mats * head_dim, hidden), f32),
                pltpu.VMEM((mats * head_dim, hidden), f32),
                pltpu.VMEM(fast_weights.shape, f32),
                pltpu.VMEM((length, width), bf16),
                pltpu.VMEM((nz, rows, columns), f32),
                pltpu.VMEM((nz, rows, columns), f32),
                pltpu.VMEM((nz, rows, columns), f32),
                dma((3, nz - 1)), dma((3, nz - 1)), dma((3,)), dma((2,)), dma((2,)), dma((2,)),
                dma((3,)), dma((3,)),
                dma((2, bits - 1)), dma((2, bits - 1)), dma((2, bits - 1)), dma((2, bits - 1)),
                dma((3,)), dma((3,)), dma((2, 3)),
                dma((nz, chunks)), dma((nz, chunks)), dma((nz, chunks)), dma((nz, chunks)),
            ],
            compiler_params=pltpu.CompilerParams(
                collective_id=0, has_side_effects=True, vmem_limit_bytes=56 * 2**20
            ),
        )(
            q_rows, k_rows, v_rows, step_sizes, fast_weights,
            norm_gain.reshape(1, -1), w_out,
        )

    return jax.shard_map(
        local,
        mesh=mesh,
        in_specs=(
            P(("seq", "head"), None),
            P(("seq", "head"), None),
            P(("seq", "head"), None),
            P("head", "seq"),
            P(None, "head", None, None),
            P("head"),
            P("head", None),
        ),
        out_specs=(P(("seq", "head"), None), P(None, "head", None, None)),
        check_vma=False,
    )
```
